768 devices in a mesh: dp: 64 (over z_lo, y, core), tensor: 12 (over z_hi, x).
Axes of the slice: x: 4, y: 8, z: 12 (z_hi: 3, z_lo: 4; z = z_hi * 4 + z_lo), core: 2. Of those that a mesh axis runs over, the one named last changes fastest.
Arguments:
- gate_pre: bfloat16 [24576, 1792], P(('dp', 'tensor')), parts along dimension 0, may hold values from -6 to 6
- up_pre: bfloat16 [24576, 1792], P(('dp', 'tensor')), parts along dimension 0, may hold values from -6 to 6
- down_weight: bfloat16 [1792, 6144], P(None, 'tensor'), may hold values from -0.125 to 0.125
- out_grad: bfloat16 [24576, 6144], P(('dp', 'tensor')), parts along dimension 0, may hold values from -6 to 6
Outputs:
- output: bfloat16 [24576, 6144], P(('dp', 'tensor')), parts along dimension 0
- gate_grad: bfloat16 [24576, 1792], P(('dp', 'tensor')), parts along dimension 0
- up_grad: bfloat16 [24576, 1792], P(('dp', 'tensor')), parts along dimension 0
- weight_grad: bfloat16 [1792, 393216], P(None, ('dp', 'tensor')), parts along dimension 1
The draws below stay inside these ranges and needn't reach their ends.
There are 64 independent parts, one for each index of `dp`. The reference program is written for one: setup_inputs(seed, part) draws one part's arguments, and reference() takes and returns one part's arrays. A program takes and returns all parts, laid end to end along the dimension named above; an argument that names none is the same for every part. Nothing has to cross between parts.
All inputs are finite; a program needn't handle non-finite values.
Results may differ from the reference program's by a relative error of at most 0.034.
Values may be sent and summed in bfloat16 or wider, within the bound.
No kernel may reach another device: no remote copies, remote signals or barrier semaphores. Data moves between devices by JAX's collectives and lax.ppermute only.
A program may use at most 32 MiB of HBM per device.

```python
import jax
import jax.numpy as jnp
from jax import lax

D = 6144
FF = 1792
TOKENS = 384
N_TENSOR = 12


def block_levels(own_key, dims, shards, least, high):
    level, own = 1.0, jax.random.fold_in(own_key, 6)
    for position, blocks in shards:
        steps = jnp.exp(jax.random.uniform(jax.random.fold_in(own, position), (blocks,), jnp.float32, least / len(shards), high / len(shards)))
        level = level * jnp.repeat(steps, dims[position] // blocks).reshape([-1 if axis == position else 1 for axis in range(len(dims))])
    return level


def noise(own_key, shape, width, limit, shards=(), kind=jnp.bfloat16):
    factor_of = block_levels(own_key, shape, shards, -0.22, 0.18) if shards else 1.0
    drawn = jax.random.normal(own_key, shape, jnp.float32) * width * factor_of
    return jnp.minimum(jnp.maximum(drawn, -limit), limit).astype(kind)


def setup_inputs(seed: int = 0, part: int = 0) -> dict:
    splits = jax.random.split(jax.random.key(seed), 5)
    part_splits = jax.random.split(jax.random.fold_in(splits[4], part), 5)
    gate_pre = noise(part_splits[0], (TOKENS, FF), 1.0, 6.0, ((0, 12),))
    up_pre = noise(part_splits[1], (TOKENS, FF), 1.0, 6.0, ((0, 12),))
    down_weight = noise(splits[2], (FF, D), FF ** -0.5, 0.125, ((1, 12),))
    out_grad = noise(part_splits[3], (TOKENS, D), 1.0, 6.0, ((0, 12),))
    return dict(gate_pre=gate_pre, up_pre=up_pre, down_weight=down_weight, out_grad=out_grad)


def reference(gate_pre, up_pre, down_weight, out_grad):
    gate_vals = gate_pre.astype(jnp.float32)
    up_vals = up_pre.astype(jnp.float32)
    sig = jax.nn.sigmoid(gate_vals)
    act = gate_vals * sig
    hidden = (act * up_vals).astype(jnp.bfloat16)
    output = jnp.dot(hidden, down_weight, preferred_element_type=jnp.float32).astype(jnp.bfloat16)
    block_width = D // N_TENSOR
    hidden_grad = jnp.zeros((out_grad.shape[0], down_weight.shape[0]), jnp.float32)
    for block in range(N_TENSOR):
        grad_block = out_grad[:, block * block_width:(block + 1) * block_width]
        weight_block = down_weight[:, block * block_width:(block + 1) * block_width]
        partial_sum = lax.dot_general(grad_block, weight_block, (((1,), (1,)), ((), ())), preferred_element_type=jnp.float32)
        rounded = lax.optimization_barrier(partial_sum.astype(jnp.bfloat16))
        hidden_grad = hidden_grad + rounded.astype(jnp.float32)
    gate_grad = (hidden_grad * up_vals * sig * (1.0 + gate_vals * (1.0 - sig))).astype(jnp.bfloat16)
    up_grad = (hidden_grad * act).astype(jnp.bfloat16)
    weight_grad = lax.dot_general(hidden, out_grad, (((0,), (0,)), ((), ())), preferred_element_type=jnp.float32).astype(jnp.bfloat16)
    return output, gate_grad, up_grad, weight_grad
```

```python
import jax
import jax.numpy as jnp
from jax import lax
from jax.sharding import PartitionSpec as P


def grad_product(block_rows, cotangent):
    return lax.dot_general(
        block_rows, cotangent, (((0,), (0,)), ((), ())), preferred_element_type=jnp.float32
    )


def body(gate_pre, up_pre, down_weight, out_grad):
    rows, hidden_width = gate_pre.shape
    width = down_weight.shape[1]
    group = out_grad.shape[1] // width
    gate_vals = gate_pre.astype(jnp.float32)
    up_vals = up_pre.astype(jnp.float32)
    sig = jax.nn.sigmoid(gate_vals)
    act = gate_vals * sig
    hidden = (act * up_vals).astype(jnp.bfloat16)

    cotangent_blocks = jnp.swapaxes(out_grad.reshape(rows, group, width), 0, 1)
    hidden_copies = jnp.broadcast_to(hidden[None], (group, rows, hidden_width))
    sent = jnp.concatenate([cotangent_blocks, hidden_copies], axis=2)
    got = lax.all_to_all(sent, "tensor", 0, 0, tiled=True)
    got = got.reshape(group * rows, width + hidden_width)
    cotangent = got[:, :width]
    hidden_all = got[:, width:]

    columns = jnp.dot(hidden_all, down_weight, preferred_element_type=jnp.float32)
    partial_sums = lax.dot_general(
        cotangent, down_weight, (((1,), (1,)), ((), ())), preferred_element_type=jnp.float32
    )
    back = jnp.concatenate(
        [columns.astype(jnp.bfloat16), partial_sums.astype(jnp.bfloat16)], axis=1
    ).reshape(group, rows, width + hidden_width)
    mine = lax.all_to_all(back, "tensor", 0, 0, tiled=True)
    output = jnp.swapaxes(mine[:, :, :width], 0, 1).reshape(rows, group * width)
    hidden_grad = jnp.sum(mine[:, :, width:].astype(jnp.float32), axis=0)

    weight_grad = grad_product(hidden_all, cotangent).astype(jnp.bfloat16)
    gate_grad = (hidden_grad * up_vals * sig * (1.0 + gate_vals * (1.0 - sig))).astype(jnp.bfloat16)
    up_grad = (hidden_grad * act).astype(jnp.bfloat16)
    return (output, gate_grad, up_grad, weight_grad)


def solution(mesh):
    return jax.shard_map(
        body,
        mesh=mesh,
        in_specs=(
            P(("dp", "tensor"), None),
            P(("dp", "tensor"), None),
            P(None, "tensor"),
            P(("dp", "tensor"), None),
        ),
        out_specs=(
            P(("dp", "tensor"), None),
            P(("dp", "tensor"), None),
            P(("dp", "tensor"), None),
            P(None, ("dp", "tensor")),
        ),
        check_vma=False,
    )
```

```python
import jax
import jax.numpy as jnp
from jax import lax
from jax.sharding import Mesh, PartitionSpec as P

PLANES = 3
GROUP = ("plane", "line")


def shift(value, axis, size, step):
    return lax.ppermute(value, axis, [(i, (i + step) % size) for i in range(size)])


def body(gate_pre, up_pre, down_weight, out_grad):
    rows, hidden_width = gate_pre.shape
    width = down_weight.shape[1]
    group = out_grad.shape[1] // width
    line = group // PLANES
    my_plane, my_line = lax.axis_index("plane"), lax.axis_index("line")

    gate_vals = gate_pre.astype(jnp.float32)
    up_vals = up_pre.astype(jnp.float32)
    sig = jax.nn.sigmoid(gate_vals)
    act = gate_vals * sig
    hidden = (act * up_vals).astype(jnp.bfloat16)

    by_plane = [hidden] + [shift(hidden, "plane", PLANES, -j) for j in range(1, PLANES)]

    blocks = jnp.swapaxes(out_grad.reshape(rows, group, width), 0, 1)
    cotangent = lax.all_to_all(blocks, GROUP, 0, 0, tiled=True)
    cotangent = cotangent.reshape(PLANES, line, rows, width)
    cotangent = jnp.roll(cotangent, (-my_plane, -my_line), (0, 1))
    cotangent = jnp.swapaxes(cotangent, 0, 1).reshape(group * rows, width)

    mine = jnp.concatenate(by_plane, axis=0)
    by_line = [mine] + [shift(mine, "line", line, -k) for k in range(1, line)]
    hidden_all = jnp.concatenate(by_line, axis=0)

    partial_sums = lax.dot_general(
        cotangent, down_weight, (((1,), (1,)), ((), ())), preferred_element_type=jnp.float32
    ).astype(jnp.bfloat16).reshape(line, PLANES * rows, hidden_width)
    line_sums = [partial_sums[0]] + [
        shift(partial_sums[k], "line", line, k) for k in range(1, line)
    ]
    line_sum = sum(s.astype(jnp.float32) for s in line_sums)
    line_sum = line_sum.astype(jnp.bfloat16).reshape(PLANES, rows, hidden_width)
    plane_sums = [line_sum[0]] + [
        shift(line_sum[j], "plane", PLANES, j) for j in range(1, PLANES)
    ]
    hidden_grad = sum(s.astype(jnp.float32) for s in plane_sums)

    columns = jnp.dot(hidden_all, down_weight, preferred_element_type=jnp.float32)
    columns = columns.astype(jnp.bfloat16).reshape(line, PLANES, rows, width)
    columns = jnp.roll(columns, (my_line, my_plane), (0, 1))
    columns = jnp.swapaxes(columns, 0, 1).reshape(group, rows, width)
    output = lax.all_to_all(columns, GROUP, 0, 0, tiled=True)
    output = jnp.swapaxes(output, 0, 1).reshape(rows, group * width)

    weight_grad = lax.dot_general(
        hidden_all, cotangent, (((0,), (0,)), ((), ())), preferred_element_type=jnp.float32
    ).astype(jnp.bfloat16)
    gate_grad = (hidden_grad * up_vals * sig * (1.0 + gate_vals * (1.0 - sig))).astype(jnp.bfloat16)
    up_grad = (hidden_grad * act).astype(jnp.bfloat16)
    return (output, gate_grad, up_grad, weight_grad)


def solution(mesh):
    tokens = ("dp",) + GROUP
    fine = Mesh(mesh.devices.reshape(mesh.shape["dp"], PLANES, -1), tokens)
    return jax.shard_map(
        body,
        mesh=fine,
        in_specs=(P(tokens, None), P(tokens, None), P(None, GROUP), P(tokens, None)),
        out_specs=(P(tokens, None), P(tokens, None), P(tokens, None), P(None, tokens)),
        check_vma=False,
    )
```

```python
import jax
import jax.numpy as jnp
from jax import lax
from jax.experimental import pallas as pl
from jax.experimental.pallas import tpu as pltpu
from jax.sharding import Mesh, PartitionSpec as P

PLANES = 3
BLOCK_COST = 40 << 20
SUM_COST = 100 << 20
GROUP = ("plane", "line")
VMEM = pl.BlockSpec(memory_space=pltpu.VMEM)
SMEM = pl.BlockSpec(memory_space=pltpu.SMEM)
CHUNK = 256


def shift(value, axis, size, step):
    return lax.ppermute(value, axis, [(i, (i + step) % size) for i in range(size)])


def planes(value, step):
    return shift(value, "plane", PLANES, step)


def exchange(value, axis):
    return lax.all_to_all(value, axis, 0, 0, tiled=True)


def together(*values):
    return lax.optimization_barrier(values)


def add_up(terms):
    return sum(t.astype(jnp.float32) for t in terms)


def whole(kernel, place, args, outs, scratch=(), flops=0, moved=1 << 20):
    return pl.pallas_call(
        kernel,
        out_shape=outs,
        in_specs=[SMEM] + [VMEM] * len(args),
        out_specs=jax.tree.map(lambda _: VMEM, outs),
        scratch_shapes=list(scratch),
        compiler_params=pltpu.CompilerParams(vmem_limit_bytes=24 << 20),
        cost_estimate=pl.CostEstimate(flops=flops, bytes_accessed=moved, transcendentals=0),
    )(place, *args)


def block_kernel(place, rows, blocks):
    width = blocks.shape[2]
    for b in range(blocks.shape[0]):
        blocks[b] = rows[:, b * width : (b + 1) * width]


def partial_kernel(place, got, weight, stay, first, second, third, ordered):
    rows = got.shape[1]
    held = PLANES * rows
    line = ordered.shape[0] // held
    for k in range(line):
        for j in range(PLANES):
            at = k * held + j * rows
            source = lax.rem(place[0] + j, PLANES) * line + lax.rem(place[1] + k, line)
            ordered[at : at + rows, :] = got[source]
    for c in range(weight.shape[0] // CHUNK):
        span = slice(c * CHUNK, (c + 1) * CHUNK)
        part = lax.dot_general(
            ordered[...],
            weight[span, :],
            (((1,), (1,)), ((), ())),
            preferred_element_type=jnp.float32,
        ).astype(jnp.bfloat16)
        for k, piece in enumerate((stay, first, second, third)):
            piece[:, span] = part[k * held : (k + 1) * held]


def column_kernel(place, own, first, second, third, weight, columns, every):
    rows = columns.shape[1]
    held = PLANES * rows
    line = every.shape[0] // held
    for k, piece in enumerate((own, first, second, third)):
        every[k * held : (k + 1) * held, :] = piece[...]
    for c in range(weight.shape[1] // CHUNK):
        span = slice(c * CHUNK, (c + 1) * CHUNK)
        part = jnp.dot(
            every[...], weight[:, span], preferred_element_type=jnp.float32
        ).astype(jnp.bfloat16)
        for k in range(line):
            for j in range(PLANES):
                at = k * held + j * rows
                owner = lax.rem(place[0] + j, PLANES) * line + lax.rem(place[1] + k, line)
                columns[owner, :, span] = part[at : at + rows]


def output_kernel(place, columns, output):
    width = columns.shape[2]
    for b in range(columns.shape[0]):
        output[:, b * width : (b + 1) * width] = columns[b]


def body(gate_pre, up_pre, down_weight, out_grad):
    rows, hidden_width = gate_pre.shape
    width = down_weight.shape[1]
    group = out_grad.shape[1] // width
    line = group // PLANES
    place = jnp.stack([lax.axis_index("plane"), lax.axis_index("line")]).astype(jnp.int32)

    def made(*shape):
        return jax.ShapeDtypeStruct(shape, jnp.bfloat16)

    gate_vals = gate_pre.astype(jnp.float32)
    up_vals = up_pre.astype(jnp.float32)
    sig = jax.nn.sigmoid(gate_vals)
    act = gate_vals * sig
    hidden = (act * up_vals).astype(jnp.bfloat16)

    hidden, out_grad = together(hidden, out_grad)
    by_plane = [hidden] + [planes(hidden, -j) for j in range(1, PLANES)]

    blocks = whole(block_kernel, place, [out_grad], made(group, rows, width), moved=BLOCK_COST)
    by_plane[1], by_plane[2], blocks = together(by_plane[1], by_plane[2], blocks)
    got = exchange(blocks, GROUP)

    mine = jnp.concatenate(by_plane, axis=0)
    by_line = [shift(mine, "line", line, -k) for k in range(1, line)]

    *sums, cotangent = whole(
        partial_kernel,
        place,
        [got, down_weight],
        [made(PLANES * rows, hidden_width)] * line + [made(group * rows, width)],
        flops=2 * group * rows * width * hidden_width,
        moved=SUM_COST,
    )
    line_sums = [sums[0]] + [shift(sums[k], "line", line, k) for k in range(1, line)]
    line_sum = [
        add_up([s[j * rows : (j + 1) * rows] for s in line_sums]).astype(jnp.bfloat16)
        for j in range(PLANES)
    ]
    hidden_grad = add_up(together(line_sum[0], planes(line_sum[1], 1), planes(line_sum[2], 2)))

    by_line = together(*by_line, sums[0])[:-1]
    columns, hidden_all = whole(
        column_kernel,
        place,
        [mine, *by_line, down_weight],
        [made(group, rows, width), made(group * rows, hidden_width)],
        flops=2 * group * rows * width * hidden_width,
        moved=4 << 20,
    )
    columns = exchange(columns, GROUP)
    weight_grad = lax.dot_general(
        hidden_all, cotangent, (((0,), (0,)), ((), ())), preferred_element_type=jnp.float32
    ).astype(jnp.bfloat16)
    output = whole(output_kernel, place, [columns], made(rows, group * width))

    gate_grad = (hidden_grad * up_vals * sig * (1.0 + gate_vals * (1.0 - sig))).astype(jnp.bfloat16)
    up_grad = (hidden_grad * act).astype(jnp.bfloat16)
    return (output, gate_grad, up_grad, weight_grad)


BLOCK_COST = 1 << 20


def solution(mesh):
    tokens = ("dp",) + GROUP
    fine = Mesh(mesh.devices.reshape(mesh.shape["dp"], PLANES, -1), tokens)
    return jax.shard_map(
        body,
        mesh=fine,
        in_specs=(P(tokens, None), P(tokens, None), P(None, GROUP), P(tokens, None)),
        out_specs=(P(tokens, None), P(tokens, None), P(tokens, None), P(None, tokens)),
        check_vma=False,
    )
```

```python
import jax
import jax.numpy as jnp
from jax import lax
from jax.experimental import pallas as pl
from jax.experimental.pallas import tpu as pltpu
from jax.sharding import Mesh, PartitionSpec as P

PLANES = 3
BLOCK_COST = 40 << 20
SUM_COST = 100 << 20
GROUP = ("plane", "line")
VMEM = pl.BlockSpec(memory_space=pltpu.VMEM)
SMEM = pl.BlockSpec(memory_space=pltpu.SMEM)
CHUNK = 256


def shift(value, axis, size, step):
    return lax.ppermute(value, axis, [(i, (i + step) % size) for i in range(size)])


def planes(value, step):
    return shift(value, "plane", PLANES, step)


def exchange(value, axis):
    return lax.all_to_all(value, axis, 0, 0, tiled=True)


def together(*values):
    return lax.optimization_barrier(values)


def add_up(terms):
    return sum(t.astype(jnp.float32) for t in terms)


def whole(kernel, place, args, outs, scratch=(), flops=0, moved=1 << 20):
    return pl.pallas_call(
        kernel,
        out_shape=outs,
        in_specs=[SMEM] + [VMEM] * len(args),
        out_specs=jax.tree.map(lambda _: VMEM, outs),
        scratch_shapes=list(scratch),
        compiler_params=pltpu.CompilerParams(vmem_limit_bytes=24 << 20),
        cost_estimate=pl.CostEstimate(flops=flops, bytes_accessed=moved, transcendentals=0),
    )(place, *args)


def block_kernel(place, rows, blocks):
    width = blocks.shape[2]
    for b in range(blocks.shape[0]):
        blocks[b] = rows[:, b * width : (b + 1) * width]


def partial_kernel(place, got, weight, stay, first, second, third, ordered):
    rows = got.shape[1]
    held = PLANES * rows
    line = ordered.shape[0] // held
    for k in range(line):
        for j in range(PLANES):
            at = k * held + j * rows
            source = lax.rem(place[0] + j, PLANES) * line + lax.rem(place[1] + k, line)
            ordered[at : at + rows, :] = got[source]
    for c in range(weight.shape[0] // CHUNK):
        span = slice(c * CHUNK, (c + 1) * CHUNK)
        part = lax.dot_general(
            ordered[...],
            weight[span, :],
            (((1,), (1,)), ((), ())),
            preferred_element_type=jnp.float32,
        ).astype(jnp.bfloat16)
        for k, piece in enumerate((stay, first, second, third)):
            piece[:, span] = part[k * held : (k + 1) * held]


def column_kernel(place, own, first, second, third, weight, stay, up_one, up_two, every):
    line, rows = stay.shape[0], stay.shape[1]
    held = PLANES * rows
    for k, piece in enumerate((own, first, second, third)):
        every[k * held : (k + 1) * held, :] = piece[...]
    for c in range(weight.shape[1] // CHUNK):
        span = slice(c * CHUNK, (c + 1) * CHUNK)
        part = jnp.dot(
            every[...], weight[:, span], preferred_element_type=jnp.float32
        ).astype(jnp.bfloat16)
        for k in range(line):
            x = lax.rem(place[1] + k, line)
            for j, dest in enumerate((stay, up_two, up_one)):
                at = k * held + j * rows
                dest[x, :, span] = part[at : at + rows]


def output_kernel(place, columns, output):
    line, width = columns.shape[0], columns.shape[3]
    for plane in range(PLANES):
        slot = lax.rem(plane - place[0] + PLANES, PLANES)
        for x in range(line):
            b = plane * line + x
            output[:, b * width : (b + 1) * width] = columns[x, slot]


def body(gate_pre, up_pre, down_weight, out_grad):
    rows, hidden_width = gate_pre.shape
    width = down_weight.shape[1]
    group = out_grad.shape[1] // width
    line = group // PLANES
    place = jnp.stack([lax.axis_index("plane"), lax.axis_index("line")]).astype(jnp.int32)

    def made(*shape):
        return jax.ShapeDtypeStruct(shape, jnp.bfloat16)

    gate_vals = gate_pre.astype(jnp.float32)
    up_vals = up_pre.astype(jnp.float32)
    sig = jax.nn.sigmoid(gate_vals)
    act = gate_vals * sig
    hidden = (act * up_vals).astype(jnp.bfloat16)

    hidden, out_grad = together(hidden, out_grad)
    by_plane = [hidden] + [planes(hidden, -j) for j in range(1, PLANES)]

    blocks = whole(block_kernel, place, [out_grad], made(group, rows, width), moved=BLOCK_COST)
    by_plane[1], by_plane[2], blocks = together(by_plane[1], by_plane[2], blocks)
    got = exchange(blocks, GROUP)

    mine = jnp.concatenate(by_plane, axis=0)
    by_line = [shift(mine, "line", line, -k) for k in range(1, line)]

    *sums, cotangent = whole(
        partial_kernel,
        place,
        [got, down_weight],
        [made(PLANES * rows, hidden_width)] * line + [made(group * rows, width)],
        flops=2 * group * rows * width * hidden_width,
        moved=SUM_COST,
    )
    line_sums = [sums[0]] + [shift(sums[k], "line", line, k) for k in range(1, line)]
    line_sum = [
        add_up([s[j * rows : (j + 1) * rows] for s in line_sums]).astype(jnp.bfloat16)
        for j in range(PLANES)
    ]

    by_line = together(*by_line, sums[0])[:-1]
    stay, up_one, up_two, hidden_all = whole(
        column_kernel,
        place,
        [mine, *by_line, down_weight],
        [made(line, rows, width)] * 3 + [made(group * rows, hidden_width)],
        flops=2 * group * rows * width * hidden_width,
        moved=4 << 20,
    )
    from_one, from_two = planes(up_one, -1), planes(up_two, -2)
    *line_sum, stay, hidden_all = together(*line_sum, stay, hidden_all)
    hidden_grad = add_up(together(line_sum[0], planes(line_sum[1], 1), planes(line_sum[2], 2)))
    columns = exchange(jnp.stack([stay, from_one, from_two], axis=1), "line")
    weight_grad = lax.dot_general(
        hidden_all, cotangent, (((0,), (0,)), ((), ())), preferred_element_type=jnp.float32
    ).astype(jnp.bfloat16)
    output = whole(output_kernel, place, [columns], made(rows, group * width))

    gate_grad = (hidden_grad * up_vals * sig * (1.0 + gate_vals * (1.0 - sig))).astype(jnp.bfloat16)
    up_grad = (hidden_grad * act).astype(jnp.bfloat16)
    return (output, gate_grad, up_grad, weight_grad)


BLOCK_COST = 1 << 20


def solution(mesh):
    tokens = ("dp",) + GROUP
    fine = Mesh(mesh.devices.reshape(mesh.shape["dp"], PLANES, -1), tokens)
    return jax.shard_map(
        body,
        mesh=fine,
        in_specs=(P(tokens, None), P(tokens, None), P(None, GROUP), P(tokens, None)),
        out_specs=(P(tokens, None), P(tokens, None), P(tokens, None), P(None, tokens)),
        check_vma=False,
    )
```

```python
import jax
import jax.numpy as jnp
from jax import lax
from jax.experimental import pallas as pl
from jax.experimental.pallas import tpu as pltpu
from jax.sharding import Mesh, PartitionSpec as P

PLANES = 3
BLOCK_COST = 40 << 20
SUM_COST = 100 << 20
GROUP = ("plane", "line")
VMEM = pl.BlockSpec(memory_space=pltpu.VMEM)
ANY = pl.BlockSpec(memory_space=pl.ANY)
HBM = pl.BlockSpec(memory_space=pltpu.HBM)
SMEM = pl.BlockSpec(memory_space=pltpu.SMEM)
CHUNK = 256


def shift(value, axis, size, step):
    return lax.ppermute(value, axis, [(i, (i + step) % size) for i in range(size)])


def planes(value, step):
    return shift(value, "plane", PLANES, step)


def exchange(value, axis):
    return lax.all_to_all(value, axis, 0, 0, tiled=True)


def together(*values):
    return lax.optimization_barrier(values)


def add_up(terms):
    return sum(t.astype(jnp.float32) for t in terms)


def whole(kernel, place, args, outs, ins=None, dests=None, scratch=(), flops=0, moved=1 << 20):
    return pl.pallas_call(
        kernel,
        out_shape=outs,
        in_specs=[SMEM] + (ins or [VMEM] * len(args)),
        out_specs=dests or jax.tree.map(lambda _: VMEM, outs),
        scratch_shapes=list(scratch),
        compiler_params=pltpu.CompilerParams(vmem_limit_bytes=24 << 20),
        cost_estimate=pl.CostEstimate(flops=flops, bytes_accessed=moved, transcendentals=0),
    )(place, *args)


def block_kernel(place, rows, blocks):
    width = blocks.shape[2]
    for b in range(blocks.shape[0]):
        blocks[b] = rows[:, b * width : (b + 1) * width]


def partial_kernel(place, got, weight, stay, first, second, third, kept, ordered, sem):
    rows = got.shape[1]
    held = PLANES * rows
    line = ordered.shape[0] // held
    for k in range(line):
        for j in range(PLANES):
            at = k * held + j * rows
            source = lax.rem(place[0] + j, PLANES) * line + lax.rem(place[1] + k, line)
            ordered[at : at + rows, :] = got[source]
    keep = pltpu.make_async_copy(ordered, kept, sem)
    keep.start()
    for c in range(weight.shape[0] // CHUNK):
        span = slice(c * CHUNK, (c + 1) * CHUNK)
        part = lax.dot_general(
            ordered[...],
            weight[span, :],
            (((1,), (1,)), ((), ())),
            preferred_element_type=jnp.float32,
        ).astype(jnp.bfloat16)
        for k, piece in enumerate((stay, first, second, third)):
            piece[:, span] = part[k * held : (k + 1) * held]
    keep.wait()


def column_kernel(place, own, first, second, third, weight, columns, kept, every, sems):
    rows = columns.shape[1]
    held = PLANES * rows
    line = every.shape[0] // held
    copies = [
        pltpu.make_async_copy(piece, every.at[pl.ds(k * held, held)], sems.at[k])
        for k, piece in enumerate((own, first, second, third))
    ]
    for copy in copies:
        copy.start()
    for copy in copies:
        copy.wait()
    keep = pltpu.make_async_copy(every, kept, sems.at[line])
    keep.start()
    for c in range(weight.shape[1] // CHUNK):
        span = slice(c * CHUNK, (c + 1) * CHUNK)
        part = jnp.dot(
            every[...], weight[:, span], preferred_element_type=jnp.float32
        ).astype(jnp.bfloat16)
        for k in range(line):
            for j in range(PLANES):
                at = k * held + j * rows
                owner = lax.rem(place[0] + j, PLANES) * line + lax.rem(place[1] + k, line)
                columns[owner, :, span] = part[at : at + rows]
    keep.wait()


def output_kernel(place, columns, output):
    width = columns.shape[2]
    for b in range(columns.shape[0]):
        output[:, b * width : (b + 1) * width] = columns[b]


def body(gate_pre, up_pre, down_weight, out_grad):
    rows, hidden_width = gate_pre.shape
    width = down_weight.shape[1]
    group = out_grad.shape[1] // width
    line = group // PLANES
    place = jnp.stack([lax.axis_index("plane"), lax.axis_index("line")]).astype(jnp.int32)

    def made(*shape):
        return jax.ShapeDtypeStruct(shape, jnp.bfloat16)

    gate_vals = gate_pre.astype(jnp.float32)
    up_vals = up_pre.astype(jnp.float32)
    sig = jax.nn.sigmoid(gate_vals)
    act = gate_vals * sig
    hidden = (act * up_vals).astype(jnp.bfloat16)

    hidden, out_grad = together(hidden, out_grad)
    by_plane = [hidden] + [planes(hidden, -j) for j in range(1, PLANES)]

    blocks = whole(block_kernel, place, [out_grad], made(group, rows, width), moved=BLOCK_COST)
    by_plane[1], by_plane[2], blocks = together(by_plane[1], by_plane[2], blocks)
    got = exchange(blocks, GROUP)

    mine = jnp.concatenate(by_plane, axis=0)
    by_line = [shift(mine, "line", line, -k) for k in range(1, line)]

    *sums, cotangent = whole(
        partial_kernel,
        place,
        [got, down_weight],
        [made(PLANES * rows, hidden_width)] * line + [made(group * rows, width)],
        dests=[VMEM] * line + [HBM],
        scratch=[pltpu.VMEM((group * rows, width), jnp.bfloat16), pltpu.SemaphoreType.DMA],
        flops=2 * group * rows * width * hidden_width,
        moved=SUM_COST,
    )
    line_sums = [sums[0]] + [shift(sums[k], "line", line, k) for k in range(1, line)]
    line_sum = [
        add_up([s[j * rows : (j + 1) * rows] for s in line_sums]).astype(jnp.bfloat16)
        for j in range(PLANES)
    ]
    hidden_grad = add_up(together(line_sum[0], planes(line_sum[1], 1), planes(line_sum[2], 2)))

    by_line = together(*by_line, sums[0])[:-1]
    columns, hidden_all = whole(
        column_kernel,
        place,
        [mine, *by_line, down_weight],
        [made(group, rows, width), made(group * rows, hidden_width)],
        ins=[ANY] * line + [VMEM],
        dests=[VMEM, HBM],
        scratch=[
            pltpu.VMEM((group * rows, hidden_width), jnp.bfloat16),
            pltpu.SemaphoreType.DMA((line + 1,)),
        ],
        flops=2 * group * rows * width * hidden_width,
        moved=4 << 20,
    )
    columns = exchange(columns, GROUP)
    weight_grad = lax.dot_general(
        hidden_all, cotangent, (((0,), (0,)), ((), ())), preferred_element_type=jnp.float32
    ).astype(jnp.bfloat16)
    output = whole(output_kernel, place, [columns], made(rows, group * width))

    gate_grad = (hidden_grad * up_vals * sig * (1.0 + gate_vals * (1.0 - sig))).astype(jnp.bfloat16)
    up_grad = (hidden_grad * act).astype(jnp.bfloat16)
    return (output, gate_grad, up_grad, weight_grad)


BLOCK_COST = 1 << 20


def solution(mesh):
    tokens = ("dp",) + GROUP
    fine = Mesh(mesh.devices.reshape(mesh.shape["dp"], PLANES, -1), tokens)
    return jax.shard_map(
        body,
        mesh=fine,
        in_specs=(P(tokens, None), P(tokens, None), P(None, GROUP), P(tokens, None)),
        out_specs=(P(tokens, None), P(tokens, None), P(tokens, None), P(None, tokens)),
        check_vma=False,
    )
```
